128 devices in a mesh: tm: 32 (over z, x, y_hi), mp: 4 (over y_lo, core).
Axes of the slice: x: 4, y: 4 (y_hi: 2, y_lo: 2; y = y_hi * 2 + y_lo), z: 4, core: 2. Of those that a mesh axis runs over, the one named last changes fastest.
Arguments:
- hidden: bfloat16 [128, 256, 3072], P('tm', None, 'mp'), may hold values from -6 to 6
- w_qkv: bfloat16 [3072, 3, 3072], P(None, None, 'mp'), may hold values from -0.109375 to 0.109375
- w_out: bfloat16 [3072, 3072], P('mp'), may hold values from -0.109375 to 0.109375
- modulation: float32 [50, 3, 3072], replicated, may hold values from -2 to 6
- levels: int32 [32], replicated, may hold values from 0 to 49, as said below
- counts: int32 [32], replicated, may hold values from 2 to 4, as said below
- entering: bfloat16 [4, 256, 3072], P(None, None, 'mp'), may hold values from -6 to 6
Outputs:
- advanced: bfloat16 [128, 256, 3072], P('tm', None, 'mp')
The draws below stay inside these ranges and needn't reach their ends.
Inputs may be any that keep to these rules, and one draw needn't show every extreme that they name: levels start at 0 with the first span, never fall along the chain and end at 49 with the last span. The live frames of a span are its first counts slots; some span is full.
All inputs are finite; a program needn't handle non-finite values.
Results may differ from the reference program's by a relative error of at most 0.013.
The reference program's roundings to bfloat16 on the way count: a program that leaves them out, or rounds other values in their place, can miss the bound.
Values may be sent and summed in bfloat16 or wider, within the bound.
A program may use at most 256 MiB of HBM per device.

```python
import jax
import jax.numpy as jnp
from jax import lax

D = 3072
HEADS = 48
HD = 64
P_SIZE = 256
F_DEV = 4
HALO = 2
LEVELS = 50
HW = 3072
SPANS = 32
FRAMES = 128
N_MP = 4


def draw_modulation(key, part):
    key = jax.random.fold_in(key, 11)
    key_rough = jax.random.fold_in(key, 1)
    rough = jnp.clip(0.5 * jax.random.normal(key_rough, (LEVELS, 3, D), jnp.float32), -2.0, 2.0)
    shift = rough[:, 0]
    scale = rough[:, 1]
    gate = rough[:, 2]
    return jnp.stack([shift, scale, gate], axis=1).astype(jnp.float32)


def draw_levels(key, part):
    key = jax.random.fold_in(key, 23)
    base = jnp.arange(SPANS, dtype=jnp.int32) * LEVELS // SPANS
    jitter = jax.random.randint(key, (SPANS,), 0, 2, jnp.int32)
    level = jnp.minimum(base + jitter, LEVELS - 1)
    level = level.at[0].set(0).at[SPANS - 1].set(LEVELS - 1)
    return lax.cummax(level, axis=0).astype(jnp.int32)


def draw_counts(key, part):
    key = jax.random.fold_in(key, 37)
    key_count, key_top, key_low = jax.random.split(key, 3)
    count = jax.random.randint(key_count, (SPANS,), HALO, F_DEV + 1, jnp.int32)
    lowest = jax.random.randint(key_low, (), 0, SPANS, jnp.int32)
    fullest = jax.random.randint(key_top, (), 0, SPANS, jnp.int32)
    count = count.at[lowest].set(HALO).at[fullest].set(F_DEV)
    return count.astype(jnp.int32)


def steps_of(rng, extent, shards, least, top_value):
    level = 1.0
    for dim, parts in shards:
        draws = jax.random.uniform(jax.random.fold_in(jax.random.fold_in(rng, 6), dim), (parts,), jnp.float32, least / len(shards), top_value / len(shards))
        level = level * jnp.repeat(jnp.exp(draws), extent[dim] // parts).reshape((-1,) + (1,) * (len(extent) - 1 - dim))
    return level


def bell_draw(own_key, extent, width, most, cuts=(), kind=jnp.bfloat16):
    loudness = steps_of(own_key, extent, cuts, -0.22, 0.18) if cuts else 1.0
    result = jax.random.normal(own_key, extent, jnp.float32) * width * loudness
    return jnp.minimum(jnp.maximum(result, -most), most).astype(kind)


def setup_inputs(seed: int = 0) -> dict:
    streams_of = jax.random.split(jax.random.key(seed), 8)
    hidden = bell_draw(streams_of[0], (FRAMES, P_SIZE, D), 1.0, 6.0, ((0, 32), (2, 4)))
    w_qkv = bell_draw(streams_of[1], (D, 3, HW), D ** -0.5, 0.109375, ((2, 4),))
    w_out = bell_draw(streams_of[2], (HW, D), HW ** -0.5, 0.109375, ((0, 4),))
    modulation = draw_modulation(jax.random.fold_in(streams_of[7], 71), 0)
    levels = draw_levels(jax.random.fold_in(streams_of[7], 71), 0)
    counts = draw_counts(jax.random.fold_in(streams_of[7], 71), 0)
    entering = bell_draw(streams_of[6], (F_DEV, P_SIZE, D), 1.0, 6.0, ((2, 4),))
    return {"hidden": hidden, "w_qkv": w_qkv, "w_out": w_out, "modulation": modulation, "levels": levels, "counts": counts, "entering": entering}


def layer_norm(rows):
    rows = rows.astype(jnp.float32)
    mean = lax.optimization_barrier(jnp.mean(rows, axis=-1, keepdims=True))
    centred = rows - mean
    spread = lax.optimization_barrier(jnp.mean(centred * centred, axis=-1, keepdims=True))
    return centred * lax.rsqrt(spread + 1e-06)

def reference(hidden, w_qkv, w_out, modulation, levels, counts, entering):
    rows = F_DEV * P_SIZE
    columns = HEADS * HD
    spanned = hidden.reshape(SPANS, F_DEV, P_SIZE, D)
    weight_all = w_qkv.reshape(D, 3 * columns)

    def project(pair):
        block, level = pair
        mod_row = modulation[level]
        shaped = (layer_norm(block) * (1.0 + mod_row[1]) + mod_row[0]).astype(jnp.bfloat16)
        proj = jnp.dot(shaped.reshape(rows, D), weight_all, preferred_element_type=jnp.float32)
        return proj.astype(jnp.bfloat16).reshape(F_DEV, P_SIZE, 3, columns)
    projected = lax.map(project, (spanned, levels))
    pairs = projected[:, :, :, 1:].reshape(FRAMES, P_SIZE, 2, columns)
    pairs = jnp.pad(pairs, ((HALO, HALO), (0, 0), (0, 0), (0, 0)))
    slots = jnp.arange(F_DEV + 2 * HALO, dtype=jnp.int32)
    group = columns // N_MP

    def attend(index):
        before = jnp.maximum(index - 1, 0)
        after = jnp.minimum(index + 1, SPANS - 1)
        prev_ok = (slots < HALO) & (index > 0) & (F_DEV - HALO + slots < counts[before])
        own_ok = (slots >= HALO) & (slots < HALO + F_DEV) & (slots - HALO < counts[index])
        next_ok = (slots >= HALO + F_DEV) & (index < SPANS - 1) & (slots - HALO - F_DEV < counts[after])
        live = jnp.repeat(prev_ok | own_ok | next_ok, P_SIZE)
        window = lax.dynamic_slice_in_dim(pairs, (index * F_DEV).astype(jnp.int32), F_DEV + 2 * HALO, 0)
        keys = window[:, :, 0].reshape(-1, HEADS, HD).astype(jnp.float32)
        values = window[:, :, 1].reshape(-1, HEADS, HD).astype(jnp.float32)
        query = projected[index][:, :, 0].reshape(rows, HEADS, HD).astype(jnp.float32)
        scores = jnp.einsum('qhd,khd->hqk', query, keys) * HD ** (-0.5)
        scores = jnp.where(live[None, None, :], scores, -1e+30)
        top = lax.optimization_barrier(jnp.max(scores, axis=-1, keepdims=True))
        expd = jnp.exp(scores - top)
        weights = (expd / lax.optimization_barrier(jnp.sum(expd, axis=-1, keepdims=True))).astype(jnp.bfloat16)
        attended = jnp.einsum('hqk,khd->qhd', weights.astype(jnp.float32), values)
        attended = attended.astype(jnp.bfloat16).reshape(rows, columns)
        mixed = jnp.zeros((rows, D), jnp.float32)
        for index_g in range(N_MP):
            term = jnp.dot(attended[:, index_g * group:(index_g + 1) * group], w_out[index_g * group:(index_g + 1) * group], preferred_element_type=jnp.float32).astype(jnp.bfloat16)
            term = lax.optimization_barrier(term)
            mixed = mixed + term.astype(jnp.float32)
        gate = modulation[levels[index], 2]
        base = spanned[index].reshape(rows, D).astype(jnp.float32)
        return (base + gate * mixed).astype(jnp.bfloat16)
    stepped = lax.map(attend, jnp.arange(SPANS, dtype=jnp.int32))
    moved = jnp.concatenate([stepped[1:], entering.reshape(1, rows, D)], axis=0)
    return moved.reshape(FRAMES, P_SIZE, D)
```

```python
import functools

import jax
import jax.numpy as jnp
from jax import lax
from jax.experimental import pallas as pl
from jax.experimental.pallas import tpu as pltpu
from jax.sharding import PartitionSpec as P

HD = 64
HALO = 2
QUAD = 256
LN_ROWS = 32
MESH = pl.DeviceIdType.MESH

OWN_CORE, OWN_Y, OWN_FWD = 0, 4, 8
N_OWN, N_FWD, N_CORE_A, N_CORE_B = 12, 14, 16, 18
P_OWN, P_Y, P_CORE_A, P_CORE_B = 20, 22, 24, 26
TERM, PRE, FIN = 28, 32, 36
N_SEM = 40


def kernel(
    chain, hid, w, w_out, mods, gate, live, out,
    x, wv, wo, shaped, qb, kb, vb, vlive, att, tsib, rsib, town, pre, rpre, fin,
    send_sem, recv_sem, w_sem, local_sem,
):
    c = lax.axis_index("tm")
    m = lax.axis_index("mp")
    sib, par, dia = m ^ 1, m ^ 2, m ^ 3
    up = lax.rem(c + 1, chain)
    down = lax.rem(c + chain - 1, chain)
    frames, tokens, part = hid.shape
    width = 4 * part
    keys = (frames + 2 * HALO) * tokens
    to_sib, to_par = (c, sib), (c, par)
    to_up, to_down = (up, par), (down, par)

    def rc(src, dst, s, dev):
        return pltpu.make_async_remote_copy(
            src_ref=src, dst_ref=dst, send_sem=send_sem.at[s], recv_sem=recv_sem.at[s],
            device_id=dev, device_id_type=MESH,
        )

    def arrived(dst, s):
        rc(dst, dst, s, to_sib).wait_recv()

    def w_copy(j):
        return pltpu.make_async_copy(
            w.at[j // 3, :, pl.ds((j % 3) * QUAD, QUAD)], wv.at[j], w_sem.at[j]
        )

    def wo_copy(g):
        return pltpu.make_async_copy(w_out.at[:, pl.ds(g * part, part)], wo.at[g], w_sem.at[9 + g])

    own_copy = pltpu.make_async_copy(hid, x.at[m, pl.ds(HALO, frames)], local_sem)
    own_copy.start()
    for j in range(9):
        w_copy(j).start()
    for g in range(4):
        wo_copy(g).start()

    barrier = pltpu.get_barrier_semaphore()
    for dev in (to_sib, to_par, to_up, to_down):
        pl.semaphore_signal(barrier, inc=1, device_id=dev, device_id_type=MESH)
    pl.semaphore_wait(barrier, 4)

    def own_core(i):
        return rc(hid.at[i], x.at[m, HALO + i], OWN_CORE + i, to_sib)

    def own_y(i):
        return rc(hid.at[i], x.at[m, HALO + i], OWN_Y + i, to_par)

    def own_fwd(i):
        return rc(x.at[par, HALO + i], x.at[par, HALO + i], OWN_FWD + i, to_sib)

    def n_own(i):
        return rc(hid.at[i], x.at[m, HALO + frames + i], N_OWN + i, to_down)

    def n_fwd(i):
        return rc(x.at[par, HALO + i], x.at[par, HALO + frames + i], N_FWD + i, to_down)

    def n_core_a(i):
        s = HALO + frames + i
        return rc(x.at[par, s], x.at[par, s], N_CORE_A + i, to_sib)

    def n_core_b(i):
        s = HALO + frames + i
        return rc(x.at[m, s], x.at[m, s], N_CORE_B + i, to_sib)

    def p_own(i):
        return rc(hid.at[frames - HALO + i], x.at[m, i], P_OWN + i, to_up)

    def p_y(i):
        return rc(x.at[par, i], x.at[par, i], P_Y + i, to_par)

    def p_core_a(i):
        return rc(x.at[par, i], x.at[par, i], P_CORE_A + i, to_sib)

    def p_core_b(i):
        return rc(x.at[m, i], x.at[m, i], P_CORE_B + i, to_sib)

    for i in range(frames):
        own_y(i).start()
        own_core(i).start()
    for i in range(HALO):
        n_own(i).start()
        p_own(i).start()
    for i in range(keys // tokens):
        vlive[pl.ds(i * tokens, tokens), :] = jnp.broadcast_to(
            live[i:i + 1, :], (tokens, 128)
        ).astype(jnp.bfloat16)
    own_copy.wait()

    def project(slot, span):
        def norm(b, carry):
            rows = pl.ds(pl.multiple_of(b * LN_ROWS, LN_ROWS), LN_ROWS)
            xs = [x[f, slot, rows, :].astype(jnp.float32) for f in range(4)]
            mean = sum(jnp.sum(v, axis=1, keepdims=True) for v in xs) * (1.0 / width)
            xs = [v - mean for v in xs]
            var = sum(jnp.sum(v * v, axis=1, keepdims=True) for v in xs) * (1.0 / width)
            r = lax.rsqrt(var + 1e-06)
            for f in range(4):
                cols = slice(f * part, (f + 1) * part)
                y = xs[f] * r * mods[span, 1:2, cols] + mods[span, 0:1, cols]
                shaped[rows, cols] = y.astype(jnp.bfloat16)
            return carry

        lax.fori_loop(0, tokens // LN_ROWS, norm, 0)
        lv = live[pl.ds(slot, 1), :]
        lv = jnp.concatenate([lv, lv], axis=1)
        rows = pl.ds(pl.multiple_of(slot * tokens, tokens), tokens)
        first = pl.ds(HALO * tokens, tokens)

        def tile(t, carry):
            k = jnp.dot(shaped[...], wv[3 + t], preferred_element_type=jnp.float32)
            kb[t, rows, :] = k.astype(jnp.bfloat16)
            k0 = kb[t, first, :].astype(jnp.float32)
            kb[t, rows, :] = jnp.where(lv > 0.5, k, k0).astype(jnp.bfloat16)
            v = jnp.dot(shaped[...], wv[6 + t], preferred_element_type=jnp.float32)
            vb[t, rows, :] = jnp.where(lv > 0.5, v, 0.0).astype(jnp.bfloat16)
            return carry

        lax.fori_loop(0, 3, tile, 0)

    def project_query(i):
        rows = pl.ds(pl.multiple_of(i * tokens, tokens), tokens)

        def tile(t, carry):
            q = jnp.dot(shaped[...], wv[t], preferred_element_type=jnp.float32)
            q = q.astype(jnp.bfloat16).astype(jnp.float32) * HD ** (-0.5)
            qb[t, rows, :] = q.astype(jnp.bfloat16)
            return carry

        lax.fori_loop(0, 3, tile, 0)

    for j in range(9):
        w_copy(j).wait()

    def gather_step(j, carry):
        slot = lax.rem(j + HALO, frames + 2 * HALO)
        span = jnp.where(j < frames, 1, jnp.where(j < frames + HALO, 2, 0))

        @pl.when(j < frames)
        def _():
            arrived(x.at[par, HALO + j], OWN_Y + j)
            own_fwd(j).start()

            @pl.when(j < HALO)
            def _():
                n_fwd(j).start()

            arrived(x.at[sib, HALO + j], OWN_CORE + j)
            arrived(x.at[dia, HALO + j], OWN_FWD + j)

        @pl.when((j >= frames) & (j < frames + HALO))
        def _():
            i = j - frames
            arrived(x.at[m, slot], N_FWD + i)
            n_core_b(i).start()
            arrived(x.at[dia, slot], N_CORE_A + i)
            arrived(x.at[sib, slot], N_CORE_B + i)

        @pl.when(j >= frames + HALO)
        def _():
            i = j - frames - HALO
            arrived(x.at[m, slot], P_Y + i)
            p_core_b(i).start()
            arrived(x.at[dia, slot], P_CORE_A + i)
            arrived(x.at[sib, slot], P_CORE_B + i)

        project(slot, span)

        @pl.when(j < frames)
        def _():
            project_query(j)

        @pl.when(j == frames - 1)
        def _():
            for i in range(HALO):
                arrived(x.at[par, i], P_OWN + i)
                p_y(i).start()
                p_core_a(i).start()
            for i in range(HALO):
                arrived(x.at[par, HALO + frames + i], N_OWN + i)
                n_core_a(i).start()

        return carry

    lax.fori_loop(0, frames + 2 * HALO, gather_step, 0)

    for g in range(4):
        wo_copy(g).wait()

    lane = lax.broadcasted_iota(jnp.int32, (1, 128), 1)
    low = lane < HD

    def attend(i):
        rows = pl.ds(pl.multiple_of(i * tokens, tokens), tokens)

        def pair(n, carry):
            t = n // 2
            for h2 in range(1):
                cols = pl.ds(pl.multiple_of((n % 2) * 128, 128), 128)
                q = qb[t, rows, cols]
                k = kb[t, :, cols]
                v = jnp.concatenate([vb[t, :, cols], vlive[...]], axis=1)
                parts = []
                for side in (low, ~low):
                    qm = jnp.where(side, q, jnp.zeros_like(q))
                    s = lax.dot_general(
                        qm, k, (((1,), (1,)), ((), ())), preferred_element_type=jnp.float32
                    )
                    top = jnp.max(s, axis=1, keepdims=True)
                    p = jnp.exp(s - top).astype(jnp.bfloat16)
                    o = jnp.dot(p, v, preferred_element_type=jnp.float32)
                    parts.append(o[:, :128] / o[:, 128:])
                att[n] = jnp.where(low, parts[0], parts[1]).astype(jnp.bfloat16)
            return carry

        lax.fori_loop(0, 6, pair, 0)

    def term(g):
        a = jnp.concatenate([att[n] for n in range(6)], axis=1)
        return jnp.dot(a, wo[g], preferred_element_type=jnp.float32).astype(jnp.bfloat16)

    def term_copy(i):
        return rc(tsib.at[i % 2], rsib.at[i], TERM + i, to_sib)

    def pre_copy(i):
        return rc(pre.at[i % 2], rpre.at[i], PRE + i, to_par)

    def fin_copy(i):
        return rc(fin.at[i % 2], out.at[i], FIN + i, to_down)

    def finish(i):
        slot = i % 2

        @pl.when(i >= 2)
        def _():
            fin_copy(i - 2).wait_send()

        arrived(rpre.at[i], PRE + i)
        mixed = (
            town[slot, 1].astype(jnp.float32)
            + rsib[i, 1].astype(jnp.float32)
            + rpre[i].astype(jnp.float32)
        )
        res = x[par, HALO + i].astype(jnp.float32) + gate[par] * mixed
        fin[slot] = res.astype(jnp.bfloat16)
        fin_copy(i).start()

    def frame(i, carry):
        slot = i % 2
        attend(i)

        @pl.when(i >= 2)
        def _():
            term_copy(i - 2).wait_send()
            pre_copy(i - 2).wait_send()

        tsib[slot, 0] = term(sib)
        tsib[slot, 1] = term(dia)
        term_copy(i).start()
        town[slot, 0] = term(m)
        town[slot, 1] = term(par)
        arrived(rsib.at[i], TERM + i)
        pre[slot] = (town[slot, 0].astype(jnp.float32) + rsib[i, 0].astype(jnp.float32)).astype(
            jnp.bfloat16
        )
        pre_copy(i).start()

        @pl.when(i >= 1)
        def _():
            finish(i - 1)

        return carry

    lax.fori_loop(0, frames, frame, 0)
    finish(frames - 1)

    for i in range(frames):
        own_y(i).wait_send()
        own_core(i).wait_send()
        own_fwd(i).wait_send()
        arrived(out.at[i], FIN + i)
    for i in range(HALO):
        for cp in (n_own, n_fwd, n_core_a, n_core_b, p_own, p_y, p_core_a, p_core_b):
            cp(i).wait_send()
    for i in range(frames - 2, frames):
        term_copy(i).wait_send()
        pre_copy(i).wait_send()
        fin_copy(i).wait_send()


def per_device(hidden, w_qkv, w_out, modulation, levels, counts, entering):
    chain = lax.axis_size("tm")
    here = lax.axis_index("tm")
    frames, tokens, part = hidden.shape
    model = w_qkv.shape[0]
    heads_w = w_qkv.shape[2]
    before = jnp.maximum(here - 1, 0)
    after = jnp.minimum(here + 1, chain - 1)
    slots = jnp.arange(frames + 2 * HALO, dtype=jnp.int32)
    prev_ok = (slots < HALO) & (here > 0) & (frames - HALO + slots < counts[before])
    own_ok = (slots >= HALO) & (slots < HALO + frames) & (slots - HALO < counts[here])
    next_ok = (
        (slots >= HALO + frames) & (here < chain - 1) & (slots - HALO - frames < counts[after])
    )
    live = jnp.broadcast_to(
        (prev_ok | own_ok | next_ok).astype(jnp.float32)[:, None], (frames + 2 * HALO, 128)
    )
    near = modulation[levels[jnp.stack([before, here, after])]]
    mods = jnp.stack([near[:, 0], 1.0 + near[:, 1]], axis=1)
    gate = near[1, 2].reshape(4, 1, part)
    n_keys = (frames + 2 * HALO) * tokens
    bf = jnp.bfloat16
    vmem = pl.BlockSpec(memory_space=pltpu.VMEM)
    hbm = pl.BlockSpec(memory_space=pl.ANY)
    moved = pl.pallas_call(
        functools.partial(kernel, chain),
        out_shape=jax.ShapeDtypeStruct((frames, tokens, part), bf),
        in_specs=[hbm, hbm, hbm, vmem, vmem, vmem],
        out_specs=hbm,
        scratch_shapes=[
            pltpu.VMEM((4, frames + 2 * HALO, tokens, part), bf),
            pltpu.VMEM((9, model, QUAD), bf),
            pltpu.VMEM((4, heads_w, part), bf),
            pltpu.VMEM((tokens, model), bf),
            pltpu.VMEM((3, frames * tokens, QUAD), bf),
            pltpu.VMEM((3, n_keys, QUAD), bf),
            pltpu.VMEM((3, n_keys, QUAD), bf),
            pltpu.VMEM((n_keys, 128), bf),
            pltpu.VMEM((6, tokens, 128), bf),
            pltpu.VMEM((2, 2, tokens, part), bf),
            pltpu.VMEM((frames, 2, tokens, part), bf),
            pltpu.VMEM((2, 2, tokens, part), bf),
            pltpu.VMEM((2, tokens, part), bf),
            pltpu.VMEM((frames, tokens, part), bf),
            pltpu.VMEM((2, tokens, part), bf),
            pltpu.SemaphoreType.DMA((N_SEM,)),
            pltpu.SemaphoreType.DMA((N_SEM,)),
            pltpu.SemaphoreType.DMA((13,)),
            pltpu.SemaphoreType.DMA,
        ],
        compiler_params=pltpu.CompilerParams(
            collective_id=0, has_side_effects=True, vmem_limit_bytes=63 * 1000 * 1000
        ),
        cost_estimate=pl.CostEstimate(
            flops=36 * 10**9, bytes_accessed=24 * 10**6, transcendentals=25 * 10**6
        ),
        name="layer",
    )(hidden, jnp.transpose(w_qkv, (1, 0, 2)), w_out, mods, gate, live)
    return jnp.where(here == chain - 1, entering, moved)


def solution(mesh):
    in_specs = (
        P("tm", None, "mp"),
        P(None, None, "mp"),
        P("mp", None),
        P(),
        P(),
        P(),
        P(None, None, "mp"),
    )
    out_specs = P("tm", None, "mp")
    return jax.shard_map(
        per_device, mesh=mesh, in_specs=in_specs, out_specs=out_specs, check_vma=False
    )
```

```python
import functools

import jax
import jax.numpy as jnp
from jax import lax
from jax.experimental import pallas as pl
from jax.experimental.pallas import tpu as pltpu
from jax.sharding import PartitionSpec as P

HD = 64
HALO = 2
QUAD = 256
LN_ROWS = 32
PIECES = 4
MESH = pl.DeviceIdType.MESH

OWN_CORE, OWN_Y, OWN_FWD = 0, 4, 8
N_OWN, N_FWD, N_CORE_A, N_CORE_B = 12, 14, 16, 18
P_OWN, P_Y, P_CORE_A, P_CORE_B = 20, 22, 24, 26
TERM, PRE, FIN = 28, 36, 52
N_SEM = 68


def kernel(
    chain, hid, w, w_out, modulation, levels, counts, entering, out,
    x, wv, wo, shaped, qb, kb, vb, vlive, att, tsib, rsib, town, pre, rpre, fin,
    table, mods, gate, live, sums, mean_b, rstd_b, s_a, s_b, p_a, p_b, fade_a, fade_b, tops, acc, total,
    send_sem, recv_sem, w_sem, local_sem,
):
    c = lax.axis_index("tm")
    m = lax.axis_index("mp")
    sib, par, dia = m ^ 1, m ^ 2, m ^ 3
    up = lax.rem(c + 1, chain)
    down = lax.rem(c + chain - 1, chain)
    frames, tokens, part = hid.shape
    width = 4 * part
    heads_w = w.shape[2]
    keys = (frames + 2 * HALO) * tokens
    to_sib, to_par = (c, sib), (c, par)
    to_up, to_down = (up, par), (down, par)

    def rc(src, dst, s, dev):
        return pltpu.make_async_remote_copy(
            src_ref=src, dst_ref=dst, send_sem=send_sem.at[s], recv_sem=recv_sem.at[s],
            device_id=dev, device_id_type=MESH,
        )

    def arrived(dst, s):
        rc(dst, dst, s, to_sib).wait_recv()

    def w_copy(j):
        return pltpu.make_async_copy(
            w.at[j // 3, :, pl.ds((j % 3) * QUAD, QUAD)], wv.at[j], w_sem.at[j]
        )

    def wo_copy(g):
        return pltpu.make_async_copy(w_out.at[:, pl.ds(g * part, part)], wo.at[g], w_sem.at[9 + g])

    own_copy = pltpu.make_async_copy(hid, x.at[m, pl.ds(0, frames)], local_sem.at[0])
    last_copy = pltpu.make_async_copy(entering, out, local_sem.at[1])

    def mod_copy(kind):
        return pltpu.make_async_copy(modulation.at[kind], table, local_sem.at[2 + kind])

    mod_copy(0).start()
    own_copy.start()
    for j in range(9):
        w_copy(j).start()
    for g in range(4):
        wo_copy(g).start()

    barrier = pltpu.get_barrier_semaphore()
    for dev in (to_sib, to_par, to_up, to_down):
        pl.semaphore_signal(barrier, inc=1, device_id=dev, device_id_type=MESH)
    pl.semaphore_wait(barrier, 4)

    def own_core(i):
        return rc(hid.at[i], x.at[m, i], OWN_CORE + i, to_sib)

    def own_y(i):
        return rc(hid.at[i], x.at[m, i], OWN_Y + i, to_par)

    def own_fwd(i):
        return rc(x.at[par, i], x.at[par, i], OWN_FWD + i, to_sib)

    def n_own(i):
        return rc(hid.at[i], x.at[m, frames + HALO + i], N_OWN + i, to_down)

    def n_fwd(i):
        return rc(x.at[par, i], x.at[par, frames + HALO + i], N_FWD + i, to_down)

    def n_core_a(i):
        s = frames + HALO + i
        return rc(x.at[par, s], x.at[par, s], N_CORE_A + i, to_sib)

    def n_core_b(i):
        s = frames + HALO + i
        return rc(x.at[m, s], x.at[m, s], N_CORE_B + i, to_sib)

    def p_own(i):
        return rc(hid.at[frames - HALO + i], x.at[m, frames + i], P_OWN + i, to_up)

    def p_y(i):
        return rc(x.at[par, frames + i], x.at[par, frames + i], P_Y + i, to_par)

    def p_core_a(i):
        return rc(x.at[par, frames + i], x.at[par, frames + i], P_CORE_A + i, to_sib)

    def p_core_b(i):
        return rc(x.at[m, frames + i], x.at[m, frames + i], P_CORE_B + i, to_sib)

    for i in range(frames):
        own_y(i).start()
        own_core(i).start()
    n_own(0).start()
    p_own(0).start()
    p_own(1).start()

    @pl.when(c == chain - 1)
    def _():
        last_copy.start()

    before, after = jnp.maximum(c - 1, 0), jnp.minimum(c + 1, chain - 1)
    for i in range(frames + 2 * HALO):
        if i < frames:
            ok = i < counts[c]
        elif i < frames + HALO:
            ok = (c > 0) & (i - HALO < counts[before])
        else:
            ok = (c < chain - 1) & (i - HALO - frames < counts[after])
        row = jnp.where(ok, jnp.ones((1, 128), jnp.float32), jnp.zeros((1, 128), jnp.float32))
        live[i:i + 1, :] = row
        vlive[pl.ds(i * tokens, tokens), :] = jnp.broadcast_to(row, (tokens, 128)).astype(
            jnp.bfloat16
        )
    for kind in range(3):
        mod_copy(kind).wait()
        for n, near in enumerate((before, c, after)):
            row = table[pl.ds(levels[near], 1), :]
            if kind < 2:
                mods[n, kind] = jnp.broadcast_to(row + float(kind), (8, width))
            elif n == 1:
                for g in range(4):
                    gate[g] = row[:, g * part:(g + 1) * part]
        if kind < 2:
            mod_copy(kind + 1).start()
    own_copy.wait()

    def project(slot, span):
        def pieces(b):
            rows = pl.ds(pl.multiple_of(b * LN_ROWS, LN_ROWS), LN_ROWS)
            for f in range(4):
                for n in range(part // 128):
                    cols = slice(n * 128, (n + 1) * 128)
                    yield f, n, rows, x[f, slot, rows, cols].astype(jnp.float32)

        def add_up(b, carry):
            acc = [jnp.zeros((LN_ROWS, 128), jnp.float32)] * 2
            for f, n, rows, v in pieces(b):
                acc[n % 2] = acc[n % 2] + v
            sums[rows, :] = acc[0] + acc[1]
            return carry

        def add_squares(b, carry):
            acc = [jnp.zeros((LN_ROWS, 128), jnp.float32)] * 2
            for f, n, rows, v in pieces(b):
                d = v - mean_b[rows, :]
                acc[n % 2] = acc[n % 2] + d * d
            sums[rows, :] = acc[0] + acc[1]
            return carry

        def modulate(b, carry):
            for f, n, rows, v in pieces(b):
                cols = slice(f * part + n * 128, f * part + (n + 1) * 128)
                scale = jnp.concatenate([mods[span, 1, :, cols]] * (LN_ROWS // 8), axis=0)
                shift = jnp.concatenate([mods[span, 0, :, cols]] * (LN_ROWS // 8), axis=0)
                y = (v - mean_b[rows, :]) * rstd_b[rows, :] * scale + shift
                shaped[rows, cols] = y.astype(jnp.bfloat16)
            return carry

        steps = tokens // LN_ROWS
        lax.fori_loop(0, steps, add_up, 0)
        mean = jnp.sum(sums[...], axis=1, keepdims=True) * (1.0 / width)
        mean_b[...] = jnp.broadcast_to(mean, (tokens, 128))
        lax.fori_loop(0, steps, add_squares, 0)
        var = jnp.sum(sums[...], axis=1, keepdims=True) * (1.0 / width)
        rstd_b[...] = jnp.broadcast_to(lax.rsqrt(var + 1e-06), (tokens, 128))
        lax.fori_loop(0, steps, modulate, 0)
        lv = live[pl.ds(slot, 1), :]
        lv = jnp.concatenate([lv, lv], axis=1)
        rows = pl.ds(pl.multiple_of(slot * tokens, tokens), tokens)
        first = pl.ds(0, tokens)

        def tile(t, carry):
            k = jnp.dot(shaped[...], wv[3 + t], preferred_element_type=jnp.float32)
            kb[t, rows, :] = k.astype(jnp.bfloat16)
            k0 = kb[t, first, :].astype(jnp.float32)
            kb[t, rows, :] = jnp.where(lv > 0.5, k, k0).astype(jnp.bfloat16)
            v = jnp.dot(shaped[...], wv[6 + t], preferred_element_type=jnp.float32)
            vb[t, rows, :] = jnp.where(lv > 0.5, v, 0.0).astype(jnp.bfloat16)
            return carry

        lax.fori_loop(0, 3, tile, 0)

    def project_query(i):
        rows = pl.ds(pl.multiple_of(i * tokens, tokens), tokens)

        def tile(t, carry):
            q = jnp.dot(shaped[...], wv[t], preferred_element_type=jnp.float32)
            q = q.astype(jnp.bfloat16).astype(jnp.float32) * HD ** (-0.5)
            qb[t, rows, :] = q.astype(jnp.bfloat16)
            return carry

        lax.fori_loop(0, 3, tile, 0)

    for j in range(9):
        w_copy(j).wait()

    def own_step(i, carry):
        arrived(x.at[par, i], OWN_Y + i)
        own_fwd(i).start()

        @pl.when(i == 0)
        def _():
            n_fwd(0).start()
            n_own(1).start()

        @pl.when(i == 1)
        def _():
            n_fwd(1).start()

        @pl.when(i == 3)
        def _():
            arrived(x.at[par, frames], P_OWN)
            p_y(0).start()
            p_core_a(0).start()

        arrived(x.at[sib, i], OWN_CORE + i)
        arrived(x.at[dia, i], OWN_FWD + i)
        project(i, 1)
        project_query(i)
        return carry

    lax.fori_loop(0, frames, own_step, 0)
    arrived(x.at[par, frames + 1], P_OWN + 1)
    p_y(1).start()
    p_core_a(1).start()

    for g in range(4):
        wo_copy(g).wait()

    lane = lax.broadcasted_iota(jnp.int32, (1, 128), 1)
    low = lane < HD

    pairs = heads_w // 128
    early = 2 * pairs
    half = keys // 2

    def item(e):
        late = e - early
        b = late // pairs
        i = jnp.where(e < early, e // pairs, jnp.where(b < 2, b, b // 2 + 1))
        kh = jnp.where(e < early, 0, jnp.where(b < 2, 1, b % 2))
        return i, kh, e % pairs

    def place(e):
        i, kh, n = item(e)
        cols = pl.ds(pl.multiple_of((n % 2) * 128, 128), 128)
        return i, kh, n, n // 2, pl.ds(pl.multiple_of(kh * half, half), half), cols

    def score(e, s_ref):
        i, kh, n, t, key_rows, cols = place(e)
        q = qb[t, pl.ds(pl.multiple_of(i * tokens, tokens), tokens), cols]
        zero = jnp.zeros_like(q)
        q = jnp.concatenate([jnp.where(low, q, zero), jnp.where(low, zero, q)], axis=0)
        s_ref[...] = lax.dot_general(
            q, kb[t, key_rows, cols], (((1,), (1,)), ((), ())), preferred_element_type=jnp.float32
        )

    def weigh(e, s_ref, p_ref, fade):
        i, kh, n = item(e)
        for r in range(0, tokens, 32):
            rows = slice(r, r + 32)
            old = tops[i % 2, rows, :]
            new, fades = old, []
            for h in range(2):
                s = s_ref[h * tokens + r:h * tokens + r + 32, :]
                mine = lane == 2 * n + h
                was = jnp.max(jnp.where(mine & (kh > 0), old, -3e38), axis=1, keepdims=True)
                top = jnp.maximum(was, jnp.max(s, axis=1, keepdims=True))
                p_ref[h * tokens + r:h * tokens + r + 32, :] = jnp.exp(s - top).astype(jnp.bfloat16)
                new = jnp.where(mine, top, new)
                fades.append(jnp.exp(was - top))
            tops[i % 2, rows, :] = new
            fade[rows, :] = jnp.where(low, fades[0], fades[1])

    def mix(e, p_ref, fade):
        i, kh, n, t, key_rows, cols = place(e)
        v = jnp.concatenate([vb[t, key_rows, cols], vlive[key_rows, :]], axis=1)
        o = jnp.dot(p_ref[...], v, preferred_element_type=jnp.float32)
        z = jnp.where(low, o[:tokens, 128:], o[tokens:, 128:])
        o = jnp.where(low, o[:tokens, :128], o[tokens:, :128])
        later = jnp.broadcast_to(kh, (1, 128)) > 0
        o = jnp.where(later, acc[i % 2, n] * fade[...], 0.0) + o
        z = jnp.where(later, total[i % 2, n] * fade[...], 0.0) + z
        acc[i % 2, n] = o
        total[i % 2, n] = z
        att[i % 2, n] = (o / z).astype(jnp.bfloat16)

    def attend(e, end):
        score(e + 1, s_b)
        weigh(e, s_a, p_a, fade_a)
        mix(jnp.maximum(e - 1, 0), p_b, fade_b)
        score(jnp.minimum(e + 2, end - 1), s_a)
        weigh(e + 1, s_b, p_b, fade_b)
        mix(e, p_a, fade_a)

    def term(g, slot):
        a = jnp.concatenate([att[slot, n] for n in range(heads_w // 128)], axis=1)
        return jnp.dot(a, wo[g], preferred_element_type=jnp.float32).astype(jnp.bfloat16)

    def term_copy(i, b):
        return rc(tsib.at[b], rsib.at[i, b], TERM + 2 * i + b, to_sib)

    size = tokens // PIECES

    def piece(h):
        return pl.ds(pl.multiple_of(h * size, size), size)

    def pre_copy(i, h):
        return rc(
            pre.at[i % 2, piece(h)], rpre.at[i, piece(h)], PRE + PIECES * i + h, to_par
        )

    def fin_copy(i, h):
        return rc(
            fin.at[i % 2, piece(h)], out.at[i, piece(h)], FIN + PIECES * i + h, to_down
        )

    def frame_terms(i):
        slot = i % 2

        @pl.when(i >= 1)
        def _():
            term_copy(i - 1, 0).wait_send()
            term_copy(i - 1, 1).wait_send()

        tsib[0] = term(sib, slot)
        term_copy(i, 0).start()
        tsib[1] = term(dia, slot)
        term_copy(i, 1).start()
        town[slot, 0] = term(m, slot)
        town[slot, 1] = term(par, slot)

    def frame_pre(i):
        slot = i % 2

        @pl.when(i >= 2)
        def _():
            for h in range(PIECES):
                pre_copy(i - 2, h).wait_send()

        arrived(rsib.at[i, 0], TERM + 2 * i)
        for h in range(PIECES):
            rows = piece(h)
            pre[slot, rows] = (
                town[slot, 0, rows].astype(jnp.float32) + rsib[i, 0, rows].astype(jnp.float32)
            ).astype(jnp.bfloat16)
            pre_copy(i, h).start()

    def frame_fin(i, h):
        slot = i % 2
        rows = piece(h)

        @pl.when((i >= 2) & (c > 0))
        def _():
            fin_copy(i - 2, h).wait_send()

        @pl.when(h == 0)
        def _():
            arrived(rsib.at[i, 1], TERM + 2 * i + 1)

        arrived(rpre.at[i, rows], PRE + PIECES * i + h)
        mixed = (
            town[slot, 1, rows].astype(jnp.float32)
            + rsib[i, 1, rows].astype(jnp.float32)
            + rpre[i, rows].astype(jnp.float32)
        )
        res = x[par, i, rows].astype(jnp.float32) + gate[par] * mixed
        fin[slot, rows] = res.astype(jnp.bfloat16)

        @pl.when(c > 0)
        def _():
            fin_copy(i, h).start()

    def early_step(u, carry):
        attend(2 * u, early)

        @pl.when(u == pairs // 2)
        def _():
            arrived(x.at[par, frames + HALO], N_OWN)
            n_core_a(0).start()
            arrived(x.at[m, frames + HALO], N_FWD)
            n_core_b(0).start()

        return carry

    score(0, s_a)
    lax.fori_loop(0, pairs, early_step, 0)

    arrived(x.at[m, frames], P_Y)
    p_core_b(0).start()

    def halo_step(j, carry):
        slot = sum(jnp.where(j == n, s, 0) for n, s in enumerate((6, 4, 5, 7)))
        is_prev = slot < frames + HALO
        i = lax.rem(slot, 2)

        @pl.when(j == 2)
        def _():
            arrived(x.at[m, frames + 1], P_Y + 1)
            p_core_b(1).start()
            arrived(x.at[par, frames + HALO + 1], N_OWN + 1)
            n_core_a(1).start()
            arrived(x.at[m, frames + HALO + 1], N_FWD + 1)
            n_core_b(1).start()

        arrived(x.at[dia, slot], jnp.where(is_prev, P_CORE_A, N_CORE_A) + i)
        arrived(x.at[sib, slot], jnp.where(is_prev, P_CORE_B, N_CORE_B) + i)
        project(slot, jnp.where(is_prev, 0, 2))
        return carry

    lax.fori_loop(0, 2 * HALO, halo_step, 0)

    def late_step(u, carry):
        attend(early + 2 * u, items)

        @pl.when(u >= 8)
        def _():
            frame_fin((u - 8) // PIECES, (u - 8) % PIECES)

        @pl.when((u == 3) | (u == 6) | (u == 12))
        def _():
            frame_terms(jnp.where(u == 3, 0, jnp.where(u == 6, 1, 2)))

        @pl.when((u == 4) | (u == 7) | (u == 13))
        def _():
            frame_pre(jnp.where(u == 4, 0, jnp.where(u == 7, 1, 2)))

        return carry

    items = 2 * frames * pairs
    score(early, s_a)
    lax.fori_loop(0, (items - early) // 2, late_step, 0)
    mix(items - 1, p_b, fade_b)
    frame_terms(frames - 1)
    frame_pre(frames - 1)

    def last_step(q, carry):
        frame_fin(q // PIECES, q % PIECES)
        return carry

    lax.fori_loop((items - early) // 2 - 8, frames * PIECES, last_step, 0)

    for i in range(frames):
        own_y(i).wait_send()
        own_core(i).wait_send()
        own_fwd(i).wait_send()
    for i in range(HALO):
        for cp in (n_own, n_fwd, n_core_a, n_core_b, p_own, p_y, p_core_a, p_core_b):
            cp(i).wait_send()
    term_copy(frames - 1, 0).wait_send()
    term_copy(frames - 1, 1).wait_send()
    for i in range(frames - 2, frames):
        for h in range(PIECES):
            pre_copy(i, h).wait_send()

    @pl.when(c > 0)
    def _():
        for i in range(frames - 2, frames):
            for h in range(PIECES):
                fin_copy(i, h).wait_send()

    @pl.when(c < chain - 1)
    def _():
        for i in range(frames):
            for h in range(PIECES):
                arrived(out.at[i, piece(h)], FIN + PIECES * i + h)

    @pl.when(c == chain - 1)
    def _():
        last_copy.wait()


def per_device(hidden, w_qkv, w_out, modulation, levels, counts, entering):
    chain = lax.axis_size("tm")
    frames, tokens, part = hidden.shape
    model = w_qkv.shape[0]
    heads_w = w_qkv.shape[2]
    n_keys = (frames + 2 * HALO) * tokens
    bf, f32 = jnp.bfloat16, jnp.float32
    smem = pl.BlockSpec(memory_space=pltpu.SMEM)
    hbm = pl.BlockSpec(memory_space=pl.ANY)
    return pl.pallas_call(
        functools.partial(kernel, chain),
        out_shape=jax.ShapeDtypeStruct((frames, tokens, part), bf),
        in_specs=[hbm, hbm, hbm, hbm, smem, smem, hbm],
        out_specs=hbm,
        scratch_shapes=[
            pltpu.VMEM((4, frames + 2 * HALO, tokens, part), bf),
            pltpu.VMEM((9, model, QUAD), bf),
            pltpu.VMEM((4, heads_w, part), bf),
            pltpu.VMEM((tokens, model), bf),
            pltpu.VMEM((3, frames * tokens, QUAD), bf),
            pltpu.VMEM((3, n_keys, QUAD), bf),
            pltpu.VMEM((3, n_keys, QUAD), bf),
            pltpu.VMEM((n_keys, 128), bf),
            pltpu.VMEM((2, heads_w // 128, tokens, 128), bf),
            pltpu.VMEM((2, tokens, part), bf),
            pltpu.VMEM((frames, 2, tokens, part), bf),
            pltpu.VMEM((2, 2, tokens, part), bf),
            pltpu.VMEM((2, tokens, part), bf),
            pltpu.VMEM((frames, tokens, part), bf),
            pltpu.VMEM((2, tokens, part), bf),
            pltpu.VMEM(modulation.shape[::2], f32),
            pltpu.VMEM((3, 2, 8, model), f32),
            pltpu.VMEM((4, 1, part), f32),
            pltpu.VMEM((frames + 2 * HALO, 128), f32),
            pltpu.VMEM((tokens, 128), f32),
            pltpu.VMEM((tokens, 128), f32),
            pltpu.VMEM((tokens, 128), f32),
            pltpu.VMEM((2 * tokens, n_keys // 2), f32),
            pltpu.VMEM((2 * tokens, n_keys // 2), f32),
            pltpu.VMEM((2 * tokens, n_keys // 2), bf),
            pltpu.VMEM((2 * tokens, n_keys // 2), bf),
            pltpu.VMEM((tokens, 128), f32),
            pltpu.VMEM((tokens, 128), f32),
            pltpu.VMEM((2, tokens, 128), f32),
            pltpu.VMEM((2, heads_w // 128, tokens, 128), f32),
            pltpu.VMEM((2, heads_w // 128, tokens, 128), f32),
            pltpu.SemaphoreType.DMA((N_SEM,)),
            pltpu.SemaphoreType.DMA((N_SEM,)),
            pltpu.SemaphoreType.DMA((13,)),
            pltpu.SemaphoreType.DMA((5,)),
        ],
        compiler_params=pltpu.CompilerParams(
            collective_id=0, has_side_effects=True, vmem_limit_bytes=66 * 1000 * 1000
        ),
        cost_estimate=pl.CostEstimate(
            flops=36 * 10**9, bytes_accessed=24 * 10**6, transcendentals=25 * 10**6
        ),
        name="layer",
    )(
        hidden, jnp.transpose(w_qkv, (1, 0, 2)), w_out, jnp.transpose(modulation, (1, 0, 2)),
        levels, counts, entering,
    )


def solution(mesh):
    in_specs = (
        P("tm", None, "mp"),
        P(None, None, "mp"),
        P("mp", None),
        P(),
        P(),
        P(),
        P(None, None, "mp"),
    )
    out_specs = P("tm", None, "mp")
    return jax.shard_map(
        per_device, mesh=mesh, in_specs=in_specs, out_specs=out_specs, check_vma=False
    )
```

```python
import functools

import jax
import jax.numpy as jnp
from jax import lax
from jax.experimental import pallas as pl
from jax.experimental.pallas import tpu as pltpu
from jax.sharding import PartitionSpec as P

HD = 64
HALO = 2
QUAD = 256
LN_ROWS = 32
PIECES = 4
MESH = pl.DeviceIdType.MESH

OWN_CORE, OWN_Y, OWN_FWD = 0, 4, 8
N_OWN, N_FWD, N_CORE_A, N_CORE_B = 12, 14, 16, 18
P_OWN, P_Y, P_CORE_A, P_CORE_B = 20, 22, 24, 26
TERM, PRE, FIN = 28, 36, 52
N_SEM = 68


def kernel(
    chain, hid, w, w_out, modulation, levels, counts, entering, out,
    x, wv, wo, shaped, qb, kb, vb, vlive, att, tsib, rsib, town, pre, rpre, fin,
    table, mods, gate, live, sums, mean_b, rstd_b, s_a, s_b, p_a, p_b, fade_a, fade_b, tops, acc, total,
    send_sem, recv_sem, w_sem, local_sem,
):
    c = lax.axis_index("tm")
    m = lax.axis_index("mp")
    sib, par, dia = m ^ 1, m ^ 2, m ^ 3
    up = lax.rem(c + 1, chain)
    down = lax.rem(c + chain - 1, chain)
    frames, tokens, part = hid.shape
    width = 4 * part
    heads_w = w.shape[2]
    keys = (frames + 2 * HALO) * tokens
    to_sib, to_par = (c, sib), (c, par)
    to_up, to_down = (up, par), (down, par)
    odd = lax.rem(c, 2)
    even = odd == 0
    near_first = HALO * (1 - odd)
    far_first = HALO * odd
    to_near = (c + 1 - 2 * odd, par)
    to_far = (jnp.where(even, down, up), par)

    def rc(src, dst, s, dev):
        return pltpu.make_async_remote_copy(
            src_ref=src, dst_ref=dst, send_sem=send_sem.at[s], recv_sem=recv_sem.at[s],
            device_id=dev, device_id_type=MESH,
        )

    def arrived(dst, s):
        rc(dst, dst, s, to_sib).wait_recv()

    def w_copy(j):
        return pltpu.make_async_copy(
            w.at[j // 3, :, pl.ds((j % 3) * QUAD, QUAD)], wv.at[j], w_sem.at[j]
        )

    def wo_copy(g):
        return pltpu.make_async_copy(w_out.at[:, pl.ds(g * part, part)], wo.at[g], w_sem.at[9 + g])

    own_copy = pltpu.make_async_copy(hid, x.at[m, pl.ds(0, frames)], local_sem.at[0])
    last_copy = pltpu.make_async_copy(entering, out, local_sem.at[1])

    def mod_copy(kind):
        return pltpu.make_async_copy(modulation.at[kind], table, local_sem.at[2 + kind])

    mod_copy(0).start()
    own_copy.start()
    for j in range(9):
        w_copy(j).start()
    for g in range(4):
        wo_copy(g).start()

    barrier = pltpu.get_barrier_semaphore()
    for dev in (to_sib, to_par, to_up, to_down):
        pl.semaphore_signal(barrier, inc=1, device_id=dev, device_id_type=MESH)
    pl.semaphore_wait(barrier, 4)

    def own_core(i):
        return rc(hid.at[i], x.at[m, i], OWN_CORE + i, to_sib)

    def own_y(i):
        return rc(hid.at[i], x.at[m, i], OWN_Y + i, to_par)

    def own_fwd(i):
        return rc(x.at[par, i], x.at[par, i], OWN_FWD + i, to_sib)

    def n_own(i):
        return rc(hid.at[near_first + i], x.at[m, frames + HALO + i], N_OWN + i, to_near)

    def n_fwd(i):
        return rc(
            x.at[par, near_first + i], x.at[par, frames + HALO + i], N_FWD + i, to_near
        )

    def n_core_a(i):
        s = frames + HALO + i
        return rc(x.at[par, s], x.at[par, s], N_CORE_A + i, to_sib)

    def n_core_b(i):
        s = frames + HALO + i
        return rc(x.at[m, s], x.at[m, s], N_CORE_B + i, to_sib)

    def p_own(i):
        return rc(hid.at[far_first + i], x.at[m, frames + i], P_OWN + i, to_far)

    def p_y(i):
        return rc(x.at[par, frames + i], x.at[par, frames + i], P_Y + i, to_par)

    def p_core_a(i):
        return rc(x.at[par, frames + i], x.at[par, frames + i], P_CORE_A + i, to_sib)

    def p_core_b(i):
        return rc(x.at[m, frames + i], x.at[m, frames + i], P_CORE_B + i, to_sib)

    for j in range(frames):
        i = lax.rem(near_first + j, frames)
        own_y(i).start()
        own_core(i).start()
    n_own(0).start()
    p_own(0).start()
    p_own(1).start()

    @pl.when(c == chain - 1)
    def _():
        last_copy.start()

    before, after = jnp.maximum(c - 1, 0), jnp.minimum(c + 1, chain - 1)
    for i in range(frames + 2 * HALO):
        if i < frames:
            ok = i < counts[c]
        else:
            k = (i - frames) % HALO
            prev_ok = (c > 0) & (frames - HALO + k < counts[before])
            next_ok = (c < chain - 1) & (k < counts[after])
            is_prev = even if i < frames + HALO else ~even
            ok = (is_prev & prev_ok) | (~is_prev & next_ok)
        row = jnp.where(ok, jnp.ones((1, 128), jnp.float32), jnp.zeros((1, 128), jnp.float32))
        live[i:i + 1, :] = row
        vlive[pl.ds(i * tokens, tokens), :] = jnp.broadcast_to(row, (tokens, 128)).astype(
            jnp.bfloat16
        )
    for kind in range(3):
        mod_copy(kind).wait()
        for n, who in enumerate((jnp.where(even, before, after), c, jnp.where(even, after, before))):
            row = table[pl.ds(levels[who], 1), :]
            if kind < 2:
                mods[n, kind] = jnp.broadcast_to(row + float(kind), (8, width))
            elif n == 1:
                for g in range(4):
                    gate[g] = row[:, g * part:(g + 1) * part]
        if kind < 2:
            mod_copy(kind + 1).start()
    own_copy.wait()

    def project(slot, span):
        def pieces(b):
            rows = pl.ds(pl.multiple_of(b * LN_ROWS, LN_ROWS), LN_ROWS)
            for f in range(4):
                for n in range(part // 128):
                    cols = slice(n * 128, (n + 1) * 128)
                    yield f, n, rows, x[f, slot, rows, cols].astype(jnp.float32)

        def add_up(b, carry):
            acc = [jnp.zeros((LN_ROWS, 128), jnp.float32)] * 2
            for f, n, rows, v in pieces(b):
                acc[n % 2] = acc[n % 2] + v
            sums[rows, :] = acc[0] + acc[1]
            return carry

        def add_squares(b, carry):
            acc = [jnp.zeros((LN_ROWS, 128), jnp.float32)] * 2
            for f, n, rows, v in pieces(b):
                d = v - mean_b[rows, :]
                acc[n % 2] = acc[n % 2] + d * d
            sums[rows, :] = acc[0] + acc[1]
            return carry

        def modulate(b, carry):
            for f, n, rows, v in pieces(b):
                cols = slice(f * part + n * 128, f * part + (n + 1) * 128)
                scale = jnp.concatenate([mods[span, 1, :, cols]] * (LN_ROWS // 8), axis=0)
                shift = jnp.concatenate([mods[span, 0, :, cols]] * (LN_ROWS // 8), axis=0)
                y = (v - mean_b[rows, :]) * rstd_b[rows, :] * scale + shift
                shaped[rows, cols] = y.astype(jnp.bfloat16)
            return carry

        steps = tokens // LN_ROWS
        lax.fori_loop(0, steps, add_up, 0)
        mean = jnp.sum(sums[...], axis=1, keepdims=True) * (1.0 / width)
        mean_b[...] = jnp.broadcast_to(mean, (tokens, 128))
        lax.fori_loop(0, steps, add_squares, 0)
        var = jnp.sum(sums[...], axis=1, keepdims=True) * (1.0 / width)
        rstd_b[...] = jnp.broadcast_to(lax.rsqrt(var + 1e-06), (tokens, 128))
        lax.fori_loop(0, steps, modulate, 0)
        lv = live[pl.ds(slot, 1), :]
        lv = jnp.concatenate([lv, lv], axis=1)
        rows = pl.ds(pl.multiple_of(slot * tokens, tokens), tokens)
        first = pl.ds(0, tokens)

        def tile(t, carry):
            k = jnp.dot(shaped[...], wv[3 + t], preferred_element_type=jnp.float32)
            kb[t, rows, :] = k.astype(jnp.bfloat16)
            k0 = kb[t, first, :].astype(jnp.float32)
            kb[t, rows, :] = jnp.where(lv > 0.5, k, k0).astype(jnp.bfloat16)
            v = jnp.dot(shaped[...], wv[6 + t], preferred_element_type=jnp.float32)
            vb[t, rows, :] = jnp.where(lv > 0.5, v, 0.0).astype(jnp.bfloat16)
            return carry

        lax.fori_loop(0, 3, tile, 0)

    def project_query(i):
        rows = pl.ds(pl.multiple_of(i * tokens, tokens), tokens)

        def tile(t, carry):
            q = jnp.dot(shaped[...], wv[t], preferred_element_type=jnp.float32)
            q = q.astype(jnp.bfloat16).astype(jnp.float32) * HD ** (-0.5)
            qb[t, rows, :] = q.astype(jnp.bfloat16)
            return carry

        lax.fori_loop(0, 3, tile, 0)

    for j in range(9):
        w_copy(j).wait()

    def own_step(j, carry):
        i = lax.rem(near_first + j, frames)
        arrived(x.at[par, i], OWN_Y + i)
        own_fwd(i).start()

        @pl.when(j == 0)
        def _():
            n_fwd(0).start()
            n_own(1).start()

        @pl.when(j == 1)
        def _():
            n_fwd(1).start()

        @pl.when(j == 3)
        def _():
            arrived(x.at[par, frames], P_OWN)
            p_y(0).start()
            p_core_a(0).start()

        arrived(x.at[sib, i], OWN_CORE + i)
        arrived(x.at[dia, i], OWN_FWD + i)
        project(i, 1)
        project_query(i)
        return carry

    lax.fori_loop(0, frames, own_step, 0)
    for i in range(HALO, frames):
        lv = jnp.concatenate([live[i:i + 1, :]] * 2, axis=1)
        for t in range(3):
            rows = slice(i * tokens, (i + 1) * tokens)
            kb[t, rows, :] = jnp.where(lv > 0.5, kb[t, rows, :], kb[t, :tokens, :])
    arrived(x.at[par, frames + 1], P_OWN + 1)
    p_y(1).start()
    p_core_a(1).start()

    for g in range(4):
        wo_copy(g).wait()

    lane = lax.broadcasted_iota(jnp.int32, (1, 128), 1)
    low = lane < HD

    pairs = heads_w // 128
    early = 2 * pairs
    half = keys // 2

    def item(e):
        late = e - early
        b = late // pairs
        i = jnp.where(e < early, e // pairs, jnp.where(b < 2, b, b // 2 + 1))
        kh = jnp.where(e < early, 0, jnp.where(b < 2, 1, b % 2))
        return i, kh, e % pairs

    def place(e):
        i, kh, n = item(e)
        cols = pl.ds(pl.multiple_of((n % 2) * 128, 128), 128)
        return i, kh, n, n // 2, pl.ds(pl.multiple_of(kh * half, half), half), cols

    def score(e, s_ref):
        i, kh, n, t, key_rows, cols = place(e)
        q = qb[t, pl.ds(pl.multiple_of(i * tokens, tokens), tokens), cols]
        zero = jnp.zeros_like(q)
        q = jnp.concatenate([jnp.where(low, q, zero), jnp.where(low, zero, q)], axis=0)
        s_ref[...] = lax.dot_general(
            q, kb[t, key_rows, cols], (((1,), (1,)), ((), ())), preferred_element_type=jnp.float32
        )

    def weigh(e, s_ref, p_ref, fade):
        i, kh, n = item(e)
        for r in range(0, tokens, 32):
            rows = slice(r, r + 32)
            old = tops[i % 2, rows, :]
            new, fades = old, []
            for h in range(2):
                s = s_ref[h * tokens + r:h * tokens + r + 32, :]
                mine = lane == 2 * n + h
                was = jnp.max(jnp.where(mine & (kh > 0), old, -3e38), axis=1, keepdims=True)
                top = jnp.maximum(was, jnp.max(s, axis=1, keepdims=True))
                p_ref[h * tokens + r:h * tokens + r + 32, :] = jnp.exp(s - top).astype(jnp.bfloat16)
                new = jnp.where(mine, top, new)
                fades.append(jnp.exp(was - top))
            tops[i % 2, rows, :] = new
            fade[rows, :] = jnp.where(low, fades[0], fades[1])

    def mix(e, p_ref, fade):
        i, kh, n, t, key_rows, cols = place(e)
        v = jnp.concatenate([vb[t, key_rows, cols], vlive[key_rows, :]], axis=1)
        o = jnp.dot(p_ref[...], v, preferred_element_type=jnp.float32)
        z = jnp.where(low, o[:tokens, 128:], o[tokens:, 128:])
        o = jnp.where(low, o[:tokens, :128], o[tokens:, :128])
        later = jnp.broadcast_to(kh, (1, 128)) > 0
        o = jnp.where(later, acc[i % 2, n] * fade[...], 0.0) + o
        z = jnp.where(later, total[i % 2, n] * fade[...], 0.0) + z
        acc[i % 2, n] = o
        total[i % 2, n] = z
        att[i % 2, n] = (o / z).astype(jnp.bfloat16)

    def attend(e, end):
        score(e + 1, s_b)
        weigh(e, s_a, p_a, fade_a)
        mix(jnp.maximum(e - 1, 0), p_b, fade_b)
        score(jnp.minimum(e + 2, end - 1), s_a)
        weigh(e + 1, s_b, p_b, fade_b)
        mix(e, p_a, fade_a)

    def term(g, slot):
        a = jnp.concatenate([att[slot, n] for n in range(heads_w // 128)], axis=1)
        return jnp.dot(a, wo[g], preferred_element_type=jnp.float32).astype(jnp.bfloat16)

    def term_copy(i, b):
        return rc(tsib.at[b], rsib.at[i, b], TERM + 2 * i + b, to_sib)

    size = tokens // PIECES

    def piece(h):
        return pl.ds(pl.multiple_of(h * size, size), size)

    def pre_copy(i, h):
        return rc(
            pre.at[i % 2, piece(h)], rpre.at[i, piece(h)], PRE + PIECES * i + h, to_par
        )

    def fin_copy(i, h):
        return rc(
            fin.at[i % 2, piece(h)], out.at[i, piece(h)], FIN + PIECES * i + h, to_down
        )

    def frame_terms(i):
        slot = i % 2

        @pl.when(i >= 1)
        def _():
            term_copy(i - 1, 0).wait_send()
            term_copy(i - 1, 1).wait_send()

        tsib[0] = term(sib, slot)
        term_copy(i, 0).start()
        tsib[1] = term(dia, slot)
        term_copy(i, 1).start()
        town[slot, 0] = term(m, slot)
        town[slot, 1] = term(par, slot)

    def frame_pre(i):
        slot = i % 2

        @pl.when(i >= 2)
        def _():
            for h in range(PIECES):
                pre_copy(i - 2, h).wait_send()

        arrived(rsib.at[i, 0], TERM + 2 * i)
        for h in range(PIECES):
            rows = piece(h)
            pre[slot, rows] = (
                town[slot, 0, rows].astype(jnp.float32) + rsib[i, 0, rows].astype(jnp.float32)
            ).astype(jnp.bfloat16)
            pre_copy(i, h).start()

    def frame_fin(i, h):
        slot = i % 2
        rows = piece(h)

        @pl.when((i >= 2) & (c > 0))
        def _():
            fin_copy(i - 2, h).wait_send()

        @pl.when(h == 0)
        def _():
            arrived(rsib.at[i, 1], TERM + 2 * i + 1)

        arrived(rpre.at[i, rows], PRE + PIECES * i + h)
        mixed = (
            town[slot, 1, rows].astype(jnp.float32)
            + rsib[i, 1, rows].astype(jnp.float32)
            + rpre[i, rows].astype(jnp.float32)
        )
        res = x[par, i, rows].astype(jnp.float32) + gate[par] * mixed
        fin[slot, rows] = res.astype(jnp.bfloat16)

        @pl.when(c > 0)
        def _():
            fin_copy(i, h).start()

    def early_step(u, carry):
        attend(2 * u, early)

        @pl.when(u == pairs // 2)
        def _():
            arrived(x.at[par, frames + HALO], N_OWN)
            n_core_a(0).start()
            arrived(x.at[m, frames + HALO], N_FWD)
            n_core_b(0).start()

        return carry

    score(0, s_a)
    lax.fori_loop(0, pairs, early_step, 0)

    arrived(x.at[m, frames], P_Y)
    p_core_b(0).start()

    def halo_step(j, carry):
        slot = sum(jnp.where(j == n, s, 0) for n, s in enumerate((6, 4, 5, 7)))
        is_prev = slot < frames + HALO
        i = lax.rem(slot, 2)

        @pl.when(j == 2)
        def _():
            arrived(x.at[m, frames + 1], P_Y + 1)
            p_core_b(1).start()
            arrived(x.at[par, frames + HALO + 1], N_OWN + 1)
            n_core_a(1).start()
            arrived(x.at[m, frames + HALO + 1], N_FWD + 1)
            n_core_b(1).start()

        arrived(x.at[dia, slot], jnp.where(is_prev, P_CORE_A, N_CORE_A) + i)
        arrived(x.at[sib, slot], jnp.where(is_prev, P_CORE_B, N_CORE_B) + i)
        project(slot, jnp.where(is_prev, 0, 2))
        return carry

    lax.fori_loop(0, 2 * HALO, halo_step, 0)

    def late_step(u, carry):
        attend(early + 2 * u, items)

        @pl.when(u >= 8)
        def _():
            frame_fin((u - 8) // PIECES, (u - 8) % PIECES)

        @pl.when((u == 3) | (u == 6) | (u == 12))
        def _():
            frame_terms(jnp.where(u == 3, 0, jnp.where(u == 6, 1, 2)))

        @pl.when((u == 4) | (u == 7) | (u == 13))
        def _():
            frame_pre(jnp.where(u == 4, 0, jnp.where(u == 7, 1, 2)))

        return carry

    items = 2 * frames * pairs
    score(early, s_a)
    lax.fori_loop(0, (items - early) // 2, late_step, 0)
    mix(items - 1, p_b, fade_b)
    frame_terms(frames - 1)
    frame_pre(frames - 1)

    def last_step(q, carry):
        frame_fin(q // PIECES, q % PIECES)
        return carry

    lax.fori_loop((items - early) // 2 - 8, frames * PIECES, last_step, 0)

    for i in range(frames):
        own_y(i).wait_send()
        own_core(i).wait_send()
        own_fwd(i).wait_send()
    for i in range(HALO):
        for cp in (n_own, n_fwd, n_core_a, n_core_b, p_own, p_y, p_core_a, p_core_b):
            cp(i).wait_send()
    term_copy(frames - 1, 0).wait_send()
    term_copy(frames - 1, 1).wait_send()
    for i in range(frames - 2, frames):
        for h in range(PIECES):
            pre_copy(i, h).wait_send()

    @pl.when(c > 0)
    def _():
        for i in range(frames - 2, frames):
            for h in range(PIECES):
                fin_copy(i, h).wait_send()

    @pl.when(c < chain - 1)
    def _():
        for i in range(frames):
            for h in range(PIECES):
                arrived(out.at[i, piece(h)], FIN + PIECES * i + h)

    @pl.when(c == chain - 1)
    def _():
        last_copy.wait()


def per_device(hidden, w_qkv, w_out, modulation, levels, counts, entering):
    chain = lax.axis_size("tm")
    frames, tokens, part = hidden.shape
    model = w_qkv.shape[0]
    heads_w = w_qkv.shape[2]
    n_keys = (frames + 2 * HALO) * tokens
    bf, f32 = jnp.bfloat16, jnp.float32
    smem = pl.BlockSpec(memory_space=pltpu.SMEM)
    hbm = pl.BlockSpec(memory_space=pl.ANY)
    return pl.pallas_call(
        functools.partial(kernel, chain),
        out_shape=jax.ShapeDtypeStruct((frames, tokens, part), bf),
        in_specs=[hbm, hbm, hbm, hbm, smem, smem, hbm],
        out_specs=hbm,
        scratch_shapes=[
            pltpu.VMEM((4, frames + 2 * HALO, tokens, part), bf),
            pltpu.VMEM((9, model, QUAD), bf),
            pltpu.VMEM((4, heads_w, part), bf),
            pltpu.VMEM((tokens, model), bf),
            pltpu.VMEM((3, frames * tokens, QUAD), bf),
            pltpu.VMEM((3, n_keys, QUAD), bf),
            pltpu.VMEM((3, n_keys, QUAD), bf),
            pltpu.VMEM((n_keys, 128), bf),
            pltpu.VMEM((2, heads_w // 128, tokens, 128), bf),
            pltpu.VMEM((2, tokens, part), bf),
            pltpu.VMEM((frames, 2, tokens, part), bf),
            pltpu.VMEM((2, 2, tokens, part), bf),
            pltpu.VMEM((2, tokens, part), bf),
            pltpu.VMEM((frames, tokens, part), bf),
            pltpu.VMEM((2, tokens, part), bf),
            pltpu.VMEM(modulation.shape[::2], f32),
            pltpu.VMEM((3, 2, 8, model), f32),
            pltpu.VMEM((4, 1, part), f32),
            pltpu.VMEM((frames + 2 * HALO, 128), f32),
            pltpu.VMEM((tokens, 128), f32),
            pltpu.VMEM((tokens, 128), f32),
            pltpu.VMEM((tokens, 128), f32),
            pltpu.VMEM((2 * tokens, n_keys // 2), f32),
            pltpu.VMEM((2 * tokens, n_keys // 2), f32),
            pltpu.VMEM((2 * tokens, n_keys // 2), bf),
            pltpu.VMEM((2 * tokens, n_keys // 2), bf),
            pltpu.VMEM((tokens, 128), f32),
            pltpu.VMEM((tokens, 128), f32),
            pltpu.VMEM((2, tokens, 128), f32),
            pltpu.VMEM((2, heads_w // 128, tokens, 128), f32),
            pltpu.VMEM((2, heads_w // 128, tokens, 128), f32),
            pltpu.SemaphoreType.DMA((N_SEM,)),
            pltpu.SemaphoreType.DMA((N_SEM,)),
            pltpu.SemaphoreType.DMA((13,)),
            pltpu.SemaphoreType.DMA((5,)),
        ],
        compiler_params=pltpu.CompilerParams(
            collective_id=0, has_side_effects=True, vmem_limit_bytes=66 * 1000 * 1000
        ),
        cost_estimate=pl.CostEstimate(
            flops=36 * 10**9, bytes_accessed=24 * 10**6, transcendentals=25 * 10**6
        ),
        name="layer",
    )(
        hidden, jnp.transpose(w_qkv, (1, 0, 2)), w_out, jnp.transpose(modulation, (1, 0, 2)),
        levels, counts, entering,
    )


def solution(mesh):
    in_specs = (
        P("tm", None, "mp"),
        P(None, None, "mp"),
        P("mp", None),
        P(),
        P(),
        P(),
        P(None, None, "mp"),
    )
    out_specs = P("tm", None, "mp")
    return jax.shard_map(
        per_device, mesh=mesh, in_specs=in_specs, out_specs=out_specs, check_vma=False
    )
```

```python
import functools

import jax
import jax.numpy as jnp
from jax import lax
from jax.experimental import pallas as pl
from jax.experimental.pallas import tpu as pltpu
from jax.sharding import PartitionSpec as P

HD = 64
HALO = 2
QUAD = 256
LN_ROWS = 32
PIECES = 4
MESH = pl.DeviceIdType.MESH

OWN_CORE, OWN_Y, OWN_FWD = 0, 4, 8
N_OWN, N_FWD, N_CORE_A, N_CORE_B = 12, 14, 16, 18
P_OWN, P_Y, P_CORE_A, P_CORE_B = 20, 22, 24, 26
TERM, PRE, FIN = 28, 36, 52
N_SEM = 68


def kernel(
    chain, hid, w, w_out, modulation, levels, counts, entering, out,
    x, wv, wo, shaped, qb, kb, vb, vlive, att, tsib, rsib, town, pre, rpre, fin,
    table, mods, gate, live, sums, mean_b, rstd_b, s_a, s_b, p_a, p_b, fade_a, fade_b, tops, acc, total,
    send_sem, recv_sem, w_sem, local_sem,
):
    c = lax.axis_index("tm")
    m = lax.axis_index("mp")
    sib, par, dia = m ^ 1, m ^ 2, m ^ 3
    up = lax.rem(c + 1, chain)
    down = lax.rem(c + chain - 1, chain)
    frames, tokens, part = hid.shape
    width = 4 * part
    heads_w = w.shape[2]
    keys = (frames + 2 * HALO) * tokens
    to_sib, to_par = (c, sib), (c, par)
    to_up, to_down = (up, par), (down, par)
    odd = lax.rem(c, 2)
    even = odd == 0
    near_first = HALO * (1 - odd)
    far_first = HALO * odd
    to_near = (c + 1 - 2 * odd, par)
    to_far = (jnp.where(even, down, up), par)

    def rc(src, dst, s, dev):
        return pltpu.make_async_remote_copy(
            src_ref=src, dst_ref=dst, send_sem=send_sem.at[s], recv_sem=recv_sem.at[s],
            device_id=dev, device_id_type=MESH,
        )

    def arrived(dst, s):
        rc(dst, dst, s, to_sib).wait_recv()

    def w_copy(j):
        return pltpu.make_async_copy(
            w.at[j // 3, :, pl.ds((j % 3) * QUAD, QUAD)], wv.at[j], w_sem.at[j]
        )

    def wo_copy(g):
        return pltpu.make_async_copy(w_out.at[:, pl.ds(g * part, part)], wo.at[g], w_sem.at[9 + g])

    own_copy = pltpu.make_async_copy(hid, x.at[m, pl.ds(0, frames)], local_sem.at[0])
    last_copy = pltpu.make_async_copy(entering, out, local_sem.at[1])

    def mod_copy(kind):
        return pltpu.make_async_copy(modulation.at[kind], table, local_sem.at[2 + kind])

    mod_copy(0).start()
    own_copy.start()
    barrier = pltpu.get_barrier_semaphore()
    for dev in (to_sib, to_par, to_up, to_down):
        pl.semaphore_signal(barrier, inc=1, device_id=dev, device_id_type=MESH)
    pl.semaphore_wait(barrier, 4)

    def own_core(i):
        return rc(hid.at[i], x.at[m, i], OWN_CORE + i, to_sib)

    def own_y(i):
        return rc(hid.at[i], x.at[m, i], OWN_Y + i, to_par)

    def own_fwd(i):
        return rc(x.at[par, i], x.at[par, i], OWN_FWD + i, to_sib)

    def n_own(i):
        return rc(hid.at[near_first + i], x.at[m, frames + HALO + i], N_OWN + i, to_near)

    def n_fwd(i):
        return rc(
            x.at[par, near_first + i], x.at[par, frames + HALO + i], N_FWD + i, to_near
        )

    def n_core_a(i):
        s = frames + HALO + i
        return rc(x.at[par, s], x.at[par, s], N_CORE_A + i, to_sib)

    def n_core_b(i):
        s = frames + HALO + i
        return rc(x.at[m, s], x.at[m, s], N_CORE_B + i, to_sib)

    def p_own(i):
        return rc(hid.at[far_first + i], x.at[m, frames + i], P_OWN + i, to_far)

    def p_y(i):
        return rc(x.at[par, frames + i], x.at[par, frames + i], P_Y + i, to_par)

    def p_core_a(i):
        return rc(x.at[par, frames + i], x.at[par, frames + i], P_CORE_A + i, to_sib)

    def p_core_b(i):
        return rc(x.at[m, frames + i], x.at[m, frames + i], P_CORE_B + i, to_sib)

    for j in range(frames):
        i = lax.rem(near_first + j, frames)
        own_y(i).start()
        own_core(i).start()
    n_own(0).start()
    p_own(0).start()
    p_own(1).start()
    for j in range(9):
        w_copy(j).start()
    for g in range(4):
        wo_copy(g).start()

    @pl.when(c == chain - 1)
    def _():
        last_copy.start()

    before, after = jnp.maximum(c - 1, 0), jnp.minimum(c + 1, chain - 1)
    for i in range(frames + 2 * HALO):
        if i < frames:
            ok = i < counts[c]
        else:
            k = (i - frames) % HALO
            prev_ok = (c > 0) & (frames - HALO + k < counts[before])
            next_ok = (c < chain - 1) & (k < counts[after])
            is_prev = even if i < frames + HALO else ~even
            ok = (is_prev & prev_ok) | (~is_prev & next_ok)
        row = jnp.where(ok, jnp.ones((1, 128), jnp.float32), jnp.zeros((1, 128), jnp.float32))
        live[i:i + 1, :] = row
        vlive[pl.ds(i * tokens, tokens), :] = jnp.broadcast_to(row, (tokens, 128)).astype(
            jnp.bfloat16
        )
    for kind in range(3):
        mod_copy(kind).wait()
        for n, who in enumerate((jnp.where(even, before, after), c, jnp.where(even, after, before))):
            row = table[pl.ds(levels[who], 1), :]
            if kind < 2:
                mods[n, kind] = jnp.broadcast_to(row + float(kind), (8, width))
            elif n == 1:
                for g in range(4):
                    gate[g] = row[:, g * part:(g + 1) * part]
        if kind < 2:
            mod_copy(kind + 1).start()
    own_copy.wait()

    def project(slot, span):
        def pieces(b):
            rows = pl.ds(pl.multiple_of(b * LN_ROWS, LN_ROWS), LN_ROWS)
            for f in range(4):
                for n in range(part // 128):
                    cols = slice(n * 128, (n + 1) * 128)
                    yield f, n, rows, x[f, slot, rows, cols].astype(jnp.float32)

        def add_up(b, carry):
            acc = [jnp.zeros((LN_ROWS, 128), jnp.float32)] * 2
            for f, n, rows, v in pieces(b):
                acc[n % 2] = acc[n % 2] + v
            sums[rows, :] = acc[0] + acc[1]
            return carry

        def add_squares(b, carry):
            acc = [jnp.zeros((LN_ROWS, 128), jnp.float32)] * 2
            for f, n, rows, v in pieces(b):
                d = v - mean_b[rows, :]
                acc[n % 2] = acc[n % 2] + d * d
            sums[rows, :] = acc[0] + acc[1]
            return carry

        def modulate(b, carry):
            for f, n, rows, v in pieces(b):
                cols = slice(f * part + n * 128, f * part + (n + 1) * 128)
                scale = jnp.concatenate([mods[span, 1, :, cols]] * (LN_ROWS // 8), axis=0)
                shift = jnp.concatenate([mods[span, 0, :, cols]] * (LN_ROWS // 8), axis=0)
                y = (v - mean_b[rows, :]) * rstd_b[rows, :] * scale + shift
                shaped[rows, cols] = y.astype(jnp.bfloat16)
            return carry

        steps = tokens // LN_ROWS
        lax.fori_loop(0, steps, add_up, 0)
        mean = jnp.sum(sums[...], axis=1, keepdims=True) * (1.0 / width)
        mean_b[...] = jnp.broadcast_to(mean, (tokens, 128))
        lax.fori_loop(0, steps, add_squares, 0)
        var = jnp.sum(sums[...], axis=1, keepdims=True) * (1.0 / width)
        rstd_b[...] = jnp.broadcast_to(lax.rsqrt(var + 1e-06), (tokens, 128))
        lax.fori_loop(0, steps, modulate, 0)
        lv = live[pl.ds(slot, 1), :]
        lv = jnp.concatenate([lv, lv], axis=1)
        rows = pl.ds(pl.multiple_of(slot * tokens, tokens), tokens)
        first = pl.ds(0, tokens)

        def tile(t, carry):
            k = jnp.dot(shaped[...], wv[3 + t], preferred_element_type=jnp.float32)
            kb[t, rows, :] = k.astype(jnp.bfloat16)
            k0 = kb[t, first, :].astype(jnp.float32)
            kb[t, rows, :] = jnp.where(lv > 0.5, k, k0).astype(jnp.bfloat16)
            v = jnp.dot(shaped[...], wv[6 + t], preferred_element_type=jnp.float32)
            vb[t, rows, :] = jnp.where(lv > 0.5, v, 0.0).astype(jnp.bfloat16)
            return carry

        lax.fori_loop(0, 3, tile, 0)

    def project_query(i):
        rows = pl.ds(pl.multiple_of(i * tokens, tokens), tokens)

        def tile(t, carry):
            q = jnp.dot(shaped[...], wv[t], preferred_element_type=jnp.float32)
            q = q.astype(jnp.bfloat16).astype(jnp.float32) * HD ** (-0.5)
            qb[t, rows, :] = q.astype(jnp.bfloat16)
            return carry

        lax.fori_loop(0, 3, tile, 0)

    for j in range(9):
        w_copy(j).wait()

    def own_step(j, carry):
        i = lax.rem(near_first + j, frames)
        arrived(x.at[par, i], OWN_Y + i)
        own_fwd(i).start()

        @pl.when(j == 0)
        def _():
            n_fwd(0).start()
            n_own(1).start()

        @pl.when(j == 1)
        def _():
            n_fwd(1).start()

        @pl.when(j == 3)
        def _():
            arrived(x.at[par, frames], P_OWN)
            p_y(0).start()
            p_core_a(0).start()

        arrived(x.at[sib, i], OWN_CORE + i)
        arrived(x.at[dia, i], OWN_FWD + i)
        project(i, 1)
        project_query(i)
        return carry

    lax.fori_loop(0, frames, own_step, 0)
    for i in range(HALO, frames):
        lv = jnp.concatenate([live[i:i + 1, :]] * 2, axis=1)
        for t in range(3):
            rows = slice(i * tokens, (i + 1) * tokens)
            kb[t, rows, :] = jnp.where(lv > 0.5, kb[t, rows, :], kb[t, :tokens, :])
    arrived(x.at[par, frames + 1], P_OWN + 1)
    p_y(1).start()
    p_core_a(1).start()

    for g in range(4):
        wo_copy(g).wait()

    lane = lax.broadcasted_iota(jnp.int32, (1, 128), 1)
    low = lane < HD

    pairs = heads_w // 128
    early = 2 * pairs
    half = keys // 2

    def item(e):
        late = e - early
        b = late // pairs
        i = jnp.where(e < early, e // pairs, jnp.where(b < 2, b, b // 2 + 1))
        kh = jnp.where(e < early, 0, jnp.where(b < 2, 1, b % 2))
        return i, kh, e % pairs

    def place(e):
        i, kh, n = item(e)
        cols = pl.ds(pl.multiple_of((n % 2) * 128, 128), 128)
        return i, kh, n, n // 2, pl.ds(pl.multiple_of(kh * half, half), half), cols

    def score(e, s_ref):
        i, kh, n, t, key_rows, cols = place(e)
        q = qb[t, pl.ds(pl.multiple_of(i * tokens, tokens), tokens), cols]
        zero = jnp.zeros_like(q)
        q = jnp.concatenate([jnp.where(low, q, zero), jnp.where(low, zero, q)], axis=0)
        s_ref[...] = lax.dot_general(
            q, kb[t, key_rows, cols], (((1,), (1,)), ((), ())), preferred_element_type=jnp.float32
        )

    def weigh(e, s_ref, p_ref, fade):
        i, kh, n = item(e)
        for r in range(0, tokens, 32):
            rows = slice(r, r + 32)
            old = tops[i % 2, rows, :]
            new, fades = old, []
            for h in range(2):
                s = s_ref[h * tokens + r:h * tokens + r + 32, :]
                mine = lane == 2 * n + h
                was = jnp.max(jnp.where(mine & (kh > 0), old, -3e38), axis=1, keepdims=True)
                top = jnp.maximum(was, jnp.max(s, axis=1, keepdims=True))
                p_ref[h * tokens + r:h * tokens + r + 32, :] = jnp.exp(s - top).astype(jnp.bfloat16)
                new = jnp.where(mine, top, new)
                fades.append(jnp.exp(was - top))
            tops[i % 2, rows, :] = new
            fade[rows, :] = jnp.where(low, fades[0], fades[1])

    def mix(e, p_ref, fade):
        i, kh, n, t, key_rows, cols = place(e)
        v = jnp.concatenate([vb[t, key_rows, cols], vlive[key_rows, :]], axis=1)
        o = jnp.dot(p_ref[...], v, preferred_element_type=jnp.float32)
        z = jnp.where(low, o[:tokens, 128:], o[tokens:, 128:])
        o = jnp.where(low, o[:tokens, :128], o[tokens:, :128])
        later = jnp.broadcast_to(kh, (1, 128)) > 0
        o = jnp.where(later, acc[i % 2, n] * fade[...], 0.0) + o
        z = jnp.where(later, total[i % 2, n] * fade[...], 0.0) + z
        acc[i % 2, n] = o
        total[i % 2, n] = z
        att[i % 2, n] = (o / z).astype(jnp.bfloat16)

    def attend(e, end):
        score(e + 1, s_b)
        weigh(e, s_a, p_a, fade_a)
        mix(jnp.maximum(e - 1, 0), p_b, fade_b)
        score(jnp.minimum(e + 2, end - 1), s_a)
        weigh(e + 1, s_b, p_b, fade_b)
        mix(e, p_a, fade_a)

    def term(g, slot):
        a = jnp.concatenate([att[slot, n] for n in range(heads_w // 128)], axis=1)
        return jnp.dot(a, wo[g], preferred_element_type=jnp.float32).astype(jnp.bfloat16)

    def term_copy(i, b):
        return rc(tsib.at[b], rsib.at[i, b], TERM + 2 * i + b, to_sib)

    size = tokens // PIECES

    def piece(h):
        return pl.ds(pl.multiple_of(h * size, size), size)

    def pre_copy(i, h):
        return rc(
            pre.at[i % 2, piece(h)], rpre.at[i, piece(h)], PRE + PIECES * i + h, to_par
        )

    def fin_copy(i, h):
        return rc(
            fin.at[i % 2, piece(h)], out.at[i, piece(h)], FIN + PIECES * i + h, to_down
        )

    def frame_terms(i):
        slot = i % 2

        @pl.when(i >= 1)
        def _():
            term_copy(i - 1, 0).wait_send()
            term_copy(i - 1, 1).wait_send()

        tsib[0] = term(sib, slot)
        term_copy(i, 0).start()
        tsib[1] = term(dia, slot)
        term_copy(i, 1).start()
        town[slot, 0] = term(m, slot)
        town[slot, 1] = term(par, slot)

    def frame_pre(i):
        slot = i % 2

        @pl.when(i >= 2)
        def _():
            for h in range(PIECES):
                pre_copy(i - 2, h).wait_send()

        arrived(rsib.at[i, 0], TERM + 2 * i)
        for h in range(PIECES):
            rows = piece(h)
            pre[slot, rows] = (
                town[slot, 0, rows].astype(jnp.float32) + rsib[i, 0, rows].astype(jnp.float32)
            ).astype(jnp.bfloat16)
            pre_copy(i, h).start()

    def frame_fin(i, h):
        slot = i % 2
        rows = piece(h)

        @pl.when((i >= 2) & (c > 0))
        def _():
            fin_copy(i - 2, h).wait_send()

        @pl.when(h == 0)
        def _():
            arrived(rsib.at[i, 1], TERM + 2 * i + 1)

        arrived(rpre.at[i, rows], PRE + PIECES * i + h)
        mixed = (
            town[slot, 1, rows].astype(jnp.float32)
            + rsib[i, 1, rows].astype(jnp.float32)
            + rpre[i, rows].astype(jnp.float32)
        )
        res = x[par, i, rows].astype(jnp.float32) + gate[par] * mixed
        fin[slot, rows] = res.astype(jnp.bfloat16)

        @pl.when(c > 0)
        def _():
            fin_copy(i, h).start()

    def early_step(u, carry):
        attend(2 * u, early)

        @pl.when(u == pairs // 2)
        def _():
            arrived(x.at[par, frames + HALO], N_OWN)
            n_core_a(0).start()
            arrived(x.at[m, frames + HALO], N_FWD)
            n_core_b(0).start()

        return carry

    score(0, s_a)
    lax.fori_loop(0, pairs, early_step, 0)

    arrived(x.at[m, frames], P_Y)
    p_core_b(0).start()

    def halo_step(j, carry):
        slot = sum(jnp.where(j == n, s, 0) for n, s in enumerate((6, 4, 5, 7)))
        is_prev = slot < frames + HALO
        i = lax.rem(slot, 2)

        @pl.when(j == 2)
        def _():
            arrived(x.at[m, frames + 1], P_Y + 1)
            p_core_b(1).start()
            arrived(x.at[par, frames + HALO + 1], N_OWN + 1)
            n_core_a(1).start()
            arrived(x.at[m, frames + HALO + 1], N_FWD + 1)
            n_core_b(1).start()

        arrived(x.at[dia, slot], jnp.where(is_prev, P_CORE_A, N_CORE_A) + i)
        arrived(x.at[sib, slot], jnp.where(is_prev, P_CORE_B, N_CORE_B) + i)
        project(slot, jnp.where(is_prev, 0, 2))
        return carry

    lax.fori_loop(0, 2 * HALO, halo_step, 0)

    def late_step(u, carry):
        attend(early + 2 * u, items)

        @pl.when(u >= 8)
        def _():
            frame_fin((u - 8) // PIECES, (u - 8) % PIECES)

        @pl.when((u == 3) | (u == 6) | (u == 12))
        def _():
            frame_terms(jnp.where(u == 3, 0, jnp.where(u == 6, 1, 2)))

        @pl.when((u == 4) | (u == 7) | (u == 13))
        def _():
            frame_pre(jnp.where(u == 4, 0, jnp.where(u == 7, 1, 2)))

        return carry

    items = 2 * frames * pairs
    score(early, s_a)
    lax.fori_loop(0, (items - early) // 2, late_step, 0)
    mix(items - 1, p_b, fade_b)
    frame_terms(frames - 1)
    frame_pre(frames - 1)

    def last_step(q, carry):
        frame_fin(q // PIECES, q % PIECES)
        return carry

    lax.fori_loop((items - early) // 2 - 8, frames * PIECES, last_step, 0)

    for i in range(frames):
        own_y(i).wait_send()
        own_core(i).wait_send()
        own_fwd(i).wait_send()
    for i in range(HALO):
        for cp in (n_own, n_fwd, n_core_a, n_core_b, p_own, p_y, p_core_a, p_core_b):
            cp(i).wait_send()
    term_copy(frames - 1, 0).wait_send()
    term_copy(frames - 1, 1).wait_send()
    for i in range(frames - 2, frames):
        for h in range(PIECES):
            pre_copy(i, h).wait_send()

    @pl.when(c > 0)
    def _():
        for i in range(frames - 2, frames):
            for h in range(PIECES):
                fin_copy(i, h).wait_send()

    @pl.when(c < chain - 1)
    def _():
        for i in range(frames):
            for h in range(PIECES):
                arrived(out.at[i, piece(h)], FIN + PIECES * i + h)

    @pl.when(c == chain - 1)
    def _():
        last_copy.wait()


def per_device(hidden, w_qkv, w_out, modulation, levels, counts, entering):
    chain = lax.axis_size("tm")
    frames, tokens, part = hidden.shape
    model = w_qkv.shape[0]
    heads_w = w_qkv.shape[2]
    n_keys = (frames + 2 * HALO) * tokens
    bf, f32 = jnp.bfloat16, jnp.float32
    smem = pl.BlockSpec(memory_space=pltpu.SMEM)
    hbm = pl.BlockSpec(memory_space=pl.ANY)
    return pl.pallas_call(
        functools.partial(kernel, chain),
        out_shape=jax.ShapeDtypeStruct((frames, tokens, part), bf),
        in_specs=[hbm, hbm, hbm, hbm, smem, smem, hbm],
        out_specs=hbm,
        scratch_shapes=[
            pltpu.VMEM((4, frames + 2 * HALO, tokens, part), bf),
            pltpu.VMEM((9, model, QUAD), bf),
            pltpu.VMEM((4, heads_w, part), bf),
            pltpu.VMEM((tokens, model), bf),
            pltpu.VMEM((3, frames * tokens, QUAD), bf),
            pltpu.VMEM((3, n_keys, QUAD), bf),
            pltpu.VMEM((3, n_keys, QUAD), bf),
            pltpu.VMEM((n_keys, 128), bf),
            pltpu.VMEM((2, heads_w // 128, tokens, 128), bf),
            pltpu.VMEM((2, tokens, part), bf),
            pltpu.VMEM((frames, 2, tokens, part), bf),
            pltpu.VMEM((2, 2, tokens, part), bf),
            pltpu.VMEM((2, tokens, part), bf),
            pltpu.VMEM((frames, tokens, part), bf),
            pltpu.VMEM((2, tokens, part), bf),
            pltpu.VMEM(modulation.shape[::2], f32),
            pltpu.VMEM((3, 2, 8, model), f32),
            pltpu.VMEM((4, 1, part), f32),
            pltpu.VMEM((frames + 2 * HALO, 128), f32),
            pltpu.VMEM((tokens, 128), f32),
            pltpu.VMEM((tokens, 128), f32),
            pltpu.VMEM((tokens, 128), f32),
            pltpu.VMEM((2 * tokens, n_keys // 2), f32),
            pltpu.VMEM((2 * tokens, n_keys // 2), f32),
            pltpu.VMEM((2 * tokens, n_keys // 2), bf),
            pltpu.VMEM((2 * tokens, n_keys // 2), bf),
            pltpu.VMEM((tokens, 128), f32),
            pltpu.VMEM((tokens, 128), f32),
            pltpu.VMEM((2, tokens, 128), f32),
            pltpu.VMEM((2, heads_w // 128, tokens, 128), f32),
            pltpu.VMEM((2, heads_w // 128, tokens, 128), f32),
            pltpu.SemaphoreType.DMA((N_SEM,)),
            pltpu.SemaphoreType.DMA((N_SEM,)),
            pltpu.SemaphoreType.DMA((13,)),
            pltpu.SemaphoreType.DMA((5,)),
        ],
        compiler_params=pltpu.CompilerParams(
            collective_id=0, has_side_effects=True, vmem_limit_bytes=66 * 1000 * 1000
        ),
        cost_estimate=pl.CostEstimate(
            flops=36 * 10**9, bytes_accessed=24 * 10**6, transcendentals=25 * 10**6
        ),
        name="layer",
    )(
        hidden, jnp.transpose(w_qkv, (1, 0, 2)), w_out, jnp.transpose(modulation, (1, 0, 2)),
        levels, counts, entering,
    )


def solution(mesh):
    in_specs = (
        P("tm", None, "mp"),
        P(None, None, "mp"),
        P("mp", None),
        P(),
        P(),
        P(),
        P(None, None, "mp"),
    )
    out_specs = P("tm", None, "mp")
    return jax.shard_map(
        per_device, mesh=mesh, in_specs=in_specs, out_specs=out_specs, check_vma=False
    )
```
